32 devices in a mesh: groups: 2 (over x), space: 16 (over z, y, core).
Axes of the slice: x: 2, y: 2, z: 4, core: 2. Of those that a mesh axis runs over, the one named last changes fastest.
Arguments:
- counts: int32 [1024, 65536], P('space', 'groups'), parts along dimension 1, may hold values from 0 to 7
- latent: float32 [32, 65536], P(None, ('groups', 'space')), parts along dimension 1, may hold values from -4 to 4
- loading: bfloat16 [32, 2048], P(None, ('groups', 'space')), parts along dimension 1, may hold values from 0.019897461 to 0.5
- background: float32 [2048], P(('groups', 'space')), parts along dimension 0, may hold values from 0.05 to 0.5
- coupling: float32 [64], P('groups'), parts along dimension 0, may hold values from 0.05 to 0.3
- tissue: int32 [65536], P('groups'), parts along dimension 0, may hold values 0 or 1
Outputs:
- grad_latent: float32 [32, 65536], P(None, ('groups', 'space')), parts along dimension 1
- grad_loading: float32 [32, 2048], P(None, ('groups', 'space')), parts along dimension 1
The draws below stay inside these ranges and needn't reach their ends.
There are 2 independent parts, one for each index of `groups`. The reference program is written for one: setup_inputs(seed, part) draws one part's arguments, and reference() takes and returns one part's arrays. A program takes and returns all parts, laid end to end along the dimension named above; each array names one. Nothing has to cross between parts.
All inputs are finite; a program needn't handle non-finite values.
Results may differ from the reference program's by a relative error of at most 0.0018.
Values may be sent and summed in bfloat16 or wider, within the bound.
No kernel may reach another device: no remote copies, remote signals or barrier semaphores. Data moves between devices by JAX's collectives and lax.ppermute only.
A program may use at most 128 MiB of HBM per device.

```python
import math
import jax
import jax.numpy as jnp
from jax import lax

FACTORS = 32
GENES = 1024
ROW_SPOTS = 2048
SPOTS = 32768


def place_ends(entries, rng, smallest, largest):
    spot = [jax.random.randint(jax.random.fold_in(rng, axis), (), 0, length) for axis, length in enumerate(entries.shape)]
    main_axis = entries.shape.index(max(entries.shape))
    next_to = spot[:main_axis] + [(spot[main_axis] + 1) % entries.shape[main_axis]] + spot[main_axis + 1:]
    return entries.at[tuple(spot)].set(smallest).at[tuple(next_to)].set(largest)


def steps_of(key, shape, pieces, least, top_value):
    gain = 1.0
    for dim, blocks in pieces:
        draws = jax.random.uniform(jax.random.fold_in(jax.random.fold_in(key, 6), dim), (blocks,), jnp.float32, least / len(pieces), top_value / len(pieces))
        gain = gain * jnp.repeat(jnp.exp(draws), shape[dim] // blocks).reshape((-1,) + (1,) * (len(shape) - 1 - dim))
    return gain


def bell_draw(rng, dims, width, limit, pieces=(), kind=jnp.bfloat16):
    array = width * jax.random.normal(rng, dims, jnp.float32)
    if pieces:
        array = array * steps_of(rng, dims, pieces, -0.22, 0.18)
    return jnp.clip(array, -limit, limit).astype(kind)


def setup_inputs(seed: int = 0, part: int = 0) -> dict:
    seeds = jax.random.split(jax.random.key(seed), 7)
    own_keys = jax.random.split(jax.random.fold_in(seeds[6], part), 7)
    counts = place_ends(jax.random.randint(own_keys[0], (GENES, SPOTS), 0, 8), jax.random.fold_in(own_keys[0], 1), 0, 7).astype(jnp.int32)
    latent = bell_draw(own_keys[1], (FACTORS, SPOTS), 1.0, 4.0, ((1, 16),), jnp.float32)
    loading = jnp.clip(jnp.exp(math.log(0.5) - 3.224016 * jax.random.uniform(own_keys[2], (FACTORS, GENES), jnp.float32) ** steps_of(own_keys[2], (FACTORS, GENES), ((1, 16),), -0.2, 0.2)), 0.019897461, 0.5).astype(jnp.bfloat16)
    background = jnp.clip(jnp.exp(math.log(0.5) - 2.3025851 * jax.random.uniform(own_keys[3], (GENES,), jnp.float32) ** steps_of(own_keys[3], (GENES,), ((0, 16),), -0.2, 0.2)), 0.05, 0.5)
    coupling = jnp.clip(jnp.exp(jax.random.uniform(own_keys[4], (FACTORS,), jnp.float32, math.log(0.05), math.log(0.3))), 0.05, 0.3)
    tissue = place_ends((jax.random.randint(own_keys[5], (SPOTS,), 0, 4) < 3).astype(jnp.int32), jax.random.fold_in(own_keys[5], 1), 0, 1)
    return {"counts": counts, "latent": latent, "loading": loading, "background": background, "coupling": coupling, "tissue": tissue}


def neighbours(values_in):
    columns = values_in.shape[1]
    padded = jnp.pad(values_in, ((0, 0), (ROW_SPOTS, ROW_SPOTS)))
    upper_row = padded[:, :columns]
    lower_row = padded[:, 2 * ROW_SPOTS:]
    column = lax.broadcasted_iota(jnp.int32, (1, columns), 1) % ROW_SPOTS
    zero_col = jnp.zeros((values_in.shape[0], 1), values_in.dtype)
    left_cell = jnp.where(column > 0, jnp.concatenate([zero_col, values_in[:, :-1]], axis=1), 0.0)
    right_cell = jnp.where(column < ROW_SPOTS - 1, jnp.concatenate([values_in[:, 1:], zero_col], axis=1), 0.0)
    return upper_row + lower_row + left_cell + right_cell


def reference(counts, latent, loading, background, coupling, tissue):
    smoothed = latent + coupling[:, None] * (neighbours(latent) - 4.0 * latent)
    factors = jax.nn.softplus(smoothed).astype(jnp.bfloat16)
    weight_of = tissue.astype(jnp.float32)
    gene_block = min(GENES, 128)
    blocks_all = GENES // gene_block
    count_blocks = counts.reshape(blocks_all, gene_block, SPOTS)
    load_blocks = jnp.transpose(loading.reshape(FACTORS, blocks_all, gene_block), (1, 0, 2))
    back_blocks = background.reshape(blocks_all, gene_block)

    def gene_step(running, block_items):
        observed, weights, offset_rows = block_items
        expected = jnp.dot(weights.T, factors, preferred_element_type=jnp.float32) + offset_rows[:, None]
        residual = (weight_of[None, :] * (1.0 - observed.astype(jnp.float32) / expected)).astype(jnp.bfloat16)
        load_sum = jnp.dot(factors, residual.T, preferred_element_type=jnp.float32)
        return running + jnp.dot(weights, residual, preferred_element_type=jnp.float32), load_sum

    spot_sum, load_parts = lax.scan(gene_step, jnp.zeros((FACTORS, SPOTS), jnp.float32), (count_blocks, load_blocks, back_blocks))
    grad_loading = jnp.transpose(load_parts, (1, 0, 2)).reshape(FACTORS, GENES) / SPOTS
    grad_smooth = spot_sum * jax.nn.sigmoid(smoothed) / GENES
    grad_latent = grad_smooth + coupling[:, None] * (neighbours(grad_smooth) - 4.0 * grad_smooth)
    return grad_latent, grad_loading
```

```python
import functools

import jax
import jax.numpy as jnp
from jax import lax
from jax.experimental import pallas as pl
from jax.experimental.pallas import tpu as pltpu
from jax.sharding import PartitionSpec as P

SPACE = "space"
MIB = 1024 * 1024
VMEM = pl.BlockSpec(memory_space=pltpu.VMEM)


def params(mib):
    return pltpu.CompilerParams(vmem_limit_bytes=mib * MIB)


def cost(flops, nbytes, trans=0):
    return pl.CostEstimate(flops=flops, bytes_accessed=nbytes, transcendentals=trans)


def split_kernel(place, counts_ref, keep_ref, send_ref, *, width):
    core = place[0]
    mine = pl.multiple_of(core * width, width)
    other = pl.multiple_of((1 - core) * width, width)
    keep_ref[0, 0] = counts_ref[:, pl.ds(mine, width)].astype(jnp.float32).astype(jnp.bfloat16)
    send_ref[0, 0] = counts_ref[:, pl.ds(other, width)].astype(jnp.float32).astype(jnp.bfloat16)


def split_counts(counts, core, row, planes, width):
    genes = counts.shape[0]
    half = jax.ShapeDtypeStruct((planes, 2, genes, width), jnp.bfloat16)
    block = pl.BlockSpec((1, 1, genes, width), lambda i, j, p: (i, lax.rem(j + p[1], 2), 0, 0))
    return pl.pallas_call(
        functools.partial(split_kernel, width=width),
        grid_spec=pltpu.PrefetchScalarGridSpec(
            num_scalar_prefetch=1,
            grid=(planes, 2),
            in_specs=[pl.BlockSpec((genes, 2 * width), lambda i, j, p: (0, 2 * i + j))],
            out_specs=[block, block],
        ),
        out_shape=[half, half],
        compiler_params=params(12),
        cost_estimate=cost(counts.size, counts.size * 6),
    )(jnp.stack([core, row]), counts)


def stencil(values, upper, lower, strength):
    width = values.shape[1]
    column = lax.broadcasted_iota(jnp.int32, values.shape, 1)
    left = jnp.where(column > 0, pltpu.roll(values, 1, 1), 0.0)
    right = jnp.where(column < width - 1, pltpu.roll(values, width - 1, 1), 0.0)
    return values + strength * (upper + lower + left + right - 4.0 * values)


def factor_kernel(latent_ref, up_ref, down_ref, strength_ref, tissue_ref, factor_ref, slope_ref, *, scale):
    smoothed = stencil(latent_ref[...], up_ref[...], down_ref[...], strength_ref[...])
    small = jnp.exp(-jnp.abs(smoothed))
    inside = tissue_ref[...] > 0
    soft = jnp.maximum(smoothed, 0.0) + jnp.log1p(small)
    factor_ref[...] = jnp.where(inside, soft, 0.0).astype(jnp.bfloat16)
    sigmoid = jnp.where(smoothed >= 0.0, 1.0, small) / (1.0 + small)
    slope_ref[...] = jnp.where(inside, sigmoid * scale, 0.0)


def gene_kernel(place, own_f, other_f, keep_ref, came_ref, weight_ref, turned_ref, back_ref, own_p, other_p, load_p, *, step):
    genes = keep_ref.shape[2]
    width = own_f.shape[1]
    weights, turned = weight_ref[...], turned_ref[...]
    offset = jnp.concatenate([back_ref[...]] * (step // 128), axis=1)
    load = jnp.zeros(load_p.shape, jnp.float32)
    for half, (field, out) in enumerate(((own_f, own_p), (other_f, other_p))):
        for at in range(0, width, step):
            f = field[:, at : at + step]
            rate = jnp.dot(turned, f, preferred_element_type=jnp.float32) + offset
            seen = jnp.concatenate(
                [keep_ref[0, half, :, at : at + step], came_ref[0, half, :, at : at + step]], axis=0
            ).astype(jnp.float32)
            residual = (1.0 - seen / rate).astype(jnp.bfloat16)
            out[:, at : at + step] = jnp.dot(weights, residual, preferred_element_type=jnp.float32).astype(out.dtype)
            load += lax.dot_general(f, residual, (((1,), (1,)), ((), ())), preferred_element_type=jnp.float32)
    load_p[...] = load


def gene_sums(plane, own_f, other_f, keep, came, weights, turned, back):
    factors, width = own_f.shape
    genes = keep.shape[2]
    whole = lambda shape: pl.BlockSpec(shape, lambda i, p: (0,) * len(shape))
    part = pl.BlockSpec((1, 2, genes, width), lambda i, p: (p[0], 0, 0, 0))
    work = 2 * genes * 2 * width
    return pl.pallas_call(
        functools.partial(gene_kernel, step=512),
        grid_spec=pltpu.PrefetchScalarGridSpec(
            num_scalar_prefetch=1,
            grid=(1,),
            in_specs=[
                whole(own_f.shape), whole(own_f.shape), part, part,
                whole(weights.shape), whole(turned.shape), whole(back.shape),
            ],
            out_specs=[whole(own_f.shape), whole(own_f.shape), whole((factors, 2 * genes))],
        ),
        out_shape=[
            jax.ShapeDtypeStruct(own_f.shape, jnp.float32),
            jax.ShapeDtypeStruct(own_f.shape, jnp.bfloat16),
            jax.ShapeDtypeStruct((factors, 2 * genes), jnp.float32),
        ],
        compiler_params=params(12),
        cost_estimate=cost(6 * factors * work, 3 * work, work),
    )(plane.reshape(1), own_f, other_f, keep, came, weights, turned, back)


def last_kernel(own_ref, up_ref, down_ref, strength_ref, out_ref):
    out_ref[...] = stencil(
        own_ref[...], up_ref[...].astype(jnp.float32), down_ref[...].astype(jnp.float32), strength_ref[...]
    )


def local(counts, latent, loading, background, coupling, tissue):
    factors, width = latent.shape
    genes, total_spots = counts.shape
    count = lax.axis_size(SPACE)
    planes = count // 4
    me = lax.axis_index(SPACE)
    core, row, plane = lax.rem(me, 2), lax.rem(me // 2, 2), me // 4

    def send(x, to):
        return lax.ppermute(x, SPACE, [(i, to(i)) for i in range(count)])

    def halo(x):
        return (
            lax.ppermute(x, SPACE, [(i, i + 1) for i in range(count - 1)]),
            lax.ppermute(x, SPACE, [(i + 1, i) for i in range(count - 1)]),
        )

    over_core = lambda i: i ^ 1
    over_row = lambda i: i ^ 2
    along = lambda s: lambda i: (i + 4 * s) % count

    up, down = halo(latent)
    both = jnp.concatenate([loading.astype(jnp.float32), background[None], jnp.zeros((7, genes), jnp.float32)])
    both = jnp.concatenate([both, send(both, over_core)], axis=1)
    weights = both[:factors].astype(jnp.bfloat16)
    turned = weights.T
    back = jnp.broadcast_to(both[factors][:, None], (2 * genes, 128))

    keep, away = split_counts(counts, core, row, planes, width)
    came = send(away, over_core)

    inside = lax.dynamic_slice(tissue, (me * width,), (width,)).reshape(1, width)
    strength = coupling.reshape(factors, 1)
    field, slope = pl.pallas_call(
        functools.partial(factor_kernel, scale=1.0 / (genes * count)),
        in_specs=[VMEM] * 5,
        out_specs=[VMEM] * 2,
        out_shape=[jax.ShapeDtypeStruct(latent.shape, jnp.bfloat16), jax.ShapeDtypeStruct(latent.shape, jnp.float32)],
        compiler_params=params(8),
        cost_estimate=cost(latent.size * 20, latent.size * 18, latent.size * 3),
    )(latent, up, down, strength, inside)

    order = sorted(range(planes), key=lambda s: min(s, planes - s))
    fields = {s: field if s == 0 else send(field, along(s)) for s in order}
    others = {s: send(fields[s], over_row) for s in order}
    total = None
    loads = None
    returned = []
    for s in order:
        source = lax.rem(plane - s + planes, planes)
        own_p, other_p, load = gene_sums(source, fields[s], others[s], keep, came, weights, turned, back)
        summed = own_p + send(other_p, over_row).astype(jnp.float32)
        loads = load if loads is None else loads + load
        if s == 0:
            total = summed
        else:
            returned.append(send(summed.astype(jnp.bfloat16), along(-s)))
    for r in returned:
        total = total + r.astype(jnp.float32)
    grad_smooth = total * slope
    up2, down2 = halo(grad_smooth.astype(jnp.bfloat16))
    grad_latent = pl.pallas_call(
        last_kernel,
        in_specs=[VMEM] * 4,
        out_specs=VMEM,
        out_shape=jax.ShapeDtypeStruct(latent.shape, jnp.float32),
        compiler_params=params(8),
        cost_estimate=cost(latent.size * 10, latent.size * 12),
    )(grad_smooth, up2, down2, strength)
    swapped = send(loads[:, genes:], over_core)
    grad_loading = (loads[:, :genes] + swapped) / total_spots
    return grad_latent, grad_loading


def solution(mesh):
    split = P(None, ("groups", SPACE))
    return jax.shard_map(
        local,
        mesh=mesh,
        in_specs=(P(SPACE, "groups"), split, split, P(("groups", SPACE)), P("groups"), P("groups")),
        out_specs=(split, split),
        check_vma=False,
    )
```

```python
import functools

import jax
import jax.numpy as jnp
from jax import lax
from jax.experimental import pallas as pl
from jax.experimental.pallas import tpu as pltpu
from jax.sharding import PartitionSpec as P

SPACE = "space"
MIB = 1024 * 1024
VMEM = pl.BlockSpec(memory_space=pltpu.VMEM)
SMEM = pl.BlockSpec(memory_space=pltpu.SMEM)


def params(mib):
    return pltpu.CompilerParams(vmem_limit_bytes=mib * MIB)


def cost(flops, nbytes, trans=0):
    return pl.CostEstimate(flops=flops, bytes_accessed=nbytes, transcendentals=trans)


def cast_kernel(place, counts_ref, out_ref, taken, arrived, *, turn):
    planes, rows, _, width = out_ref.shape
    parity = lax.rem(place[0] + turn, 2)
    copies = []
    for block in range(planes * rows):
        start = pl.multiple_of((2 * block + parity) * width, width)
        copies.append(pltpu.make_async_copy(counts_ref.at[:, pl.ds(start, width)], taken.at[block], arrived.at[block]))
        copies[-1].start()
    for block, copy in enumerate(copies):
        copy.wait()
        out_ref[block // rows, block % rows] = taken[block].astype(jnp.float32).astype(jnp.bfloat16)


def cast_counts(place, counts, planes, width, turn):
    genes = counts.shape[0]
    return pl.pallas_call(
        functools.partial(cast_kernel, turn=turn),
        in_specs=[SMEM, pl.BlockSpec(memory_space=pltpu.HBM)],
        out_specs=VMEM,
        out_shape=jax.ShapeDtypeStruct((planes, 2, genes, width), jnp.bfloat16),
        scratch_shapes=[pltpu.VMEM((2 * planes, genes, width), jnp.int32), pltpu.SemaphoreType.DMA((2 * planes,))],
        compiler_params=params(14),
        cost_estimate=cost(counts.size, counts.size * 3),
    )(place, counts)


def column(row_ref, rows, lanes):
    tile = jnp.broadcast_to(row_ref[...], (128, rows)).T
    return jnp.concatenate([tile] * (lanes // 128), axis=1)


def stencil(values, near, far, strength):
    width = values.shape[1]
    at = lax.broadcasted_iota(jnp.int32, values.shape, 1)
    left = jnp.where(at > 0, pltpu.roll(values, 1, 1), 0.0)
    right = jnp.where(at < width - 1, pltpu.roll(values, width - 1, 1), 0.0)
    return values + strength * (near + far + left + right - 4.0 * values)


def factor_kernel(
    place, latent_ref, near_ref, far_ref, strength_ref, tissue_ref, own_w, other_w, own_b, other_b,
    factor_ref, slope_ref, weight_ref, turned_ref, back_ref, *, scale,
):
    factors, width = latent_ref.shape
    strength = column(strength_ref, factors, width)
    smoothed = stencil(latent_ref[...], near_ref[...], far_ref[...], strength)
    small = jnp.exp(-jnp.abs(smoothed))
    inside = tissue_ref[:, pl.ds(pl.multiple_of(place[3] * width, width), width)] > 0
    soft = jnp.maximum(smoothed, 0.0) + jnp.log1p(small)
    factor_ref[...] = jnp.where(inside, soft, 0.0).astype(jnp.bfloat16)
    sigmoid = jnp.where(smoothed >= 0.0, 1.0, small) / (1.0 + small)
    slope_ref[...] = jnp.where(inside, sigmoid * scale, 0.0)
    weights = jnp.concatenate([own_w[...].astype(jnp.float32), other_w[...].astype(jnp.float32)], axis=1)
    weight_ref[...] = weights.astype(jnp.bfloat16)
    turned_ref[...] = weights.T.astype(jnp.bfloat16)
    genes = own_w.shape[1]
    back_ref[:genes] = column(own_b, genes, 128)
    back_ref[genes:] = column(other_b, genes, 128)


def gene_kernel(
    place, own_f, other_f, keep_ref, came_ref, weight_ref, turned_ref, back_ref, own_p, other_p, load_p, *, step, shift,
):
    width = own_f.shape[1]
    planes = keep_ref.shape[0]
    weights, turned = weight_ref[...], turned_ref[...]
    offset = jnp.concatenate([back_ref[...]] * (step // 128), axis=1)
    load = jnp.zeros(load_p.shape, jnp.float32)
    plane = lax.rem(place[2] + planes - shift, planes)
    for half, (field, out) in enumerate(((own_f, own_p), (other_f, other_p))):
        row = lax.rem(place[1] + half, 2)
        for at in range(0, width, step):
            f = field[:, at : at + step]
            rate = jnp.dot(turned, f, preferred_element_type=jnp.float32) + offset
            seen = jnp.concatenate(
                [keep_ref[plane, row, :, at : at + step], came_ref[plane, row, :, at : at + step]], axis=0
            ).astype(jnp.float32)
            residual = (1.0 - seen / rate).astype(jnp.bfloat16)
            out[:, at : at + step] = jnp.dot(weights, residual, preferred_element_type=jnp.float32).astype(out.dtype)
            load += lax.dot_general(f, residual, (((1,), (1,)), ((), ())), preferred_element_type=jnp.float32)
    load_p[...] = load


def gene_sums(place, shift, own_f, other_f, keep, came, weights, turned, back):
    factors, width = own_f.shape
    genes = keep.shape[2]
    work = 2 * genes * 2 * width
    return pl.pallas_call(
        functools.partial(gene_kernel, step=1024, shift=shift),
        in_specs=[SMEM] + [VMEM] * 7,
        out_specs=[VMEM] * 3,
        out_shape=[
            jax.ShapeDtypeStruct(own_f.shape, jnp.float32),
            jax.ShapeDtypeStruct(own_f.shape, jnp.bfloat16),
            jax.ShapeDtypeStruct((factors, 2 * genes), jnp.float32),
        ],
        compiler_params=params(12),
        cost_estimate=cost(6 * factors * work, 3 * work, work),
    )(place, own_f, other_f, keep, came, weights, turned, back)


def last_kernel(own_ref, near_ref, far_ref, strength_ref, out_ref):
    factors, width = own_ref.shape
    out_ref[...] = stencil(
        own_ref[...], near_ref[...].astype(jnp.float32), far_ref[...].astype(jnp.float32),
        column(strength_ref, factors, width),
    )


def after(x, *done):
    return lax.optimization_barrier((x, *done))[0]


def local(counts, latent, loading, background, coupling, tissue):
    factors, width = latent.shape
    genes, total_spots = counts.shape
    count = lax.axis_size(SPACE)
    planes = count // 4
    me = lax.axis_index(SPACE)
    place = jnp.stack([me & 1, (me >> 1) & 1, me >> 2, me])

    def send(x, to):
        return lax.ppermute(x, SPACE, [(i, to(i)) for i in range(count)])

    def across(i):
        return i + 1 if i % 2 else i - 1

    def chips(x):
        return lax.ppermute(x, SPACE, [(i, across(i)) for i in range(count) if 0 <= across(i) < count])

    over_core = lambda i: i ^ 1
    over_row = lambda i: i ^ 2
    along = lambda s: lambda i: (i + 4 * s) % count

    far = chips(latent)
    near = send(latent, over_core)
    away = cast_counts(place, counts, planes, width, 1)
    other_w, other_b = send(loading, over_core), send(background, over_core)
    came = send(away, over_core)
    strength = coupling.reshape(1, factors)
    full = jax.ShapeDtypeStruct
    field, slope, weights, turned, back = pl.pallas_call(
        functools.partial(factor_kernel, scale=1.0 / (genes * count)),
        in_specs=[SMEM] + [VMEM] * 9,
        out_specs=[VMEM] * 5,
        out_shape=[
            full(latent.shape, jnp.bfloat16), full(latent.shape, jnp.float32),
            full((factors, 2 * genes), jnp.bfloat16), full((2 * genes, factors), jnp.bfloat16),
            full((2 * genes, 128), jnp.float32),
        ],
        compiler_params=params(8),
        cost_estimate=cost(latent.size * 20, latent.size * 18, latent.size * 3),
    )(
        place, latent, near, far, strength, tissue.reshape(1, total_spots),
        loading, other_w, background.reshape(1, genes), other_b.reshape(1, genes),
    )

    keep = cast_counts(after(place, field), counts, planes, width, 0)
    order = [0] + sorted(range(1, planes), key=lambda s: -min(s, planes - s))
    fields = {s: field if s == 0 else send(field, along(s)) for s in order}
    total = loads = None
    done, returned = [], []
    for at, s in enumerate(order):
        mine = fields[s] if s == 0 else after(fields[s], done[max(0, at - 2)])
        other = send(mine, over_row)
        own_p, other_p, load = gene_sums(place, s, mine, other, keep, came, weights, turned, back)
        done.append(load)
        loads = load if loads is None else loads + load
        if s == 0:
            total, later = own_p, other_p
        else:
            summed = own_p + send(other_p, over_row).astype(jnp.float32)
            returned.append(send(summed.astype(jnp.bfloat16), along(-s)))
    total = total + send(after(later, done[-2]), over_row).astype(jnp.float32)
    for r in returned:
        total = total + r.astype(jnp.float32)
    grad_smooth = total * slope
    rounded = grad_smooth.astype(jnp.bfloat16)
    near2, far2 = send(rounded, over_core), chips(rounded)
    grad_latent = pl.pallas_call(
        last_kernel,
        in_specs=[VMEM] * 4,
        out_specs=VMEM,
        out_shape=full(latent.shape, jnp.float32),
        compiler_params=params(8),
        cost_estimate=cost(latent.size * 10, latent.size * 12),
    )(grad_smooth, near2, far2, strength)
    swapped = send(loads[:, genes:], over_core)
    grad_loading = (loads[:, :genes] + swapped) / total_spots
    return grad_latent, grad_loading


def solution(mesh):
    split = P(None, ("groups", SPACE))
    return jax.shard_map(
        local,
        mesh=mesh,
        in_specs=(P(SPACE, "groups"), split, split, P(("groups", SPACE)), P("groups"), P("groups")),
        out_specs=(split, split),
        check_vma=False,
    )
```

```python
import functools

import jax
import jax.numpy as jnp
from jax import lax
from jax.experimental import pallas as pl
from jax.experimental.pallas import tpu as pltpu
from jax.sharding import PartitionSpec as P

SPACE = "space"
MIB = 1024 * 1024
VMEM = pl.BlockSpec(memory_space=pltpu.VMEM)
SMEM = pl.BlockSpec(memory_space=pltpu.SMEM)


def params(mib):
    return pltpu.CompilerParams(vmem_limit_bytes=mib * MIB)


def cost(flops, nbytes, trans=0):
    return pl.CostEstimate(flops=flops, bytes_accessed=nbytes, transcendentals=trans)


def cast_kernel(place, counts_ref, out_ref, taken, arrived, *, turn):
    planes, rows, _, width = out_ref.shape
    parity = lax.rem(place[0] + turn, 2)
    copies = []
    for block in range(planes * rows):
        start = pl.multiple_of((2 * block + parity) * width, width)
        copies.append(pltpu.make_async_copy(counts_ref.at[:, pl.ds(start, width)], taken.at[block], arrived.at[block]))
        copies[-1].start()
    for block, copy in enumerate(copies):
        copy.wait()
        out_ref[block // rows, block % rows] = taken[block].astype(jnp.float32).astype(jnp.bfloat16)


def cast_counts(place, counts, planes, width, turn):
    genes = counts.shape[0]
    return pl.pallas_call(
        functools.partial(cast_kernel, turn=turn),
        in_specs=[SMEM, pl.BlockSpec(memory_space=pltpu.HBM)],
        out_specs=VMEM,
        out_shape=jax.ShapeDtypeStruct((planes, 2, genes, width), jnp.bfloat16),
        scratch_shapes=[pltpu.VMEM((2 * planes, genes, width), jnp.int32), pltpu.SemaphoreType.DMA((2 * planes,))],
        compiler_params=params(14),
        cost_estimate=cost(counts.size, counts.size * 3),
    )(place, counts)


def column(row_ref, rows, lanes):
    tile = jnp.broadcast_to(row_ref[...], (128, rows)).T
    return jnp.concatenate([tile] * (lanes // 128), axis=1)


def stencil(values, near, far, strength):
    width = values.shape[1]
    at = lax.broadcasted_iota(jnp.int32, values.shape, 1)
    left = jnp.where(at > 0, pltpu.roll(values, 1, 1), 0.0)
    right = jnp.where(at < width - 1, pltpu.roll(values, width - 1, 1), 0.0)
    return values + strength * (near + far + left + right - 4.0 * values)


def factor_kernel(
    place, latent_ref, near_ref, far_ref, strength_ref, tissue_ref, own_w, other_w, own_b, other_b,
    factor_ref, slope_ref, weight_ref, turned_ref, back_ref, *, scale,
):
    factors, width = latent_ref.shape
    strength = column(strength_ref, factors, width)
    smoothed = stencil(latent_ref[...], near_ref[...], far_ref[...], strength)
    small = jnp.exp(-jnp.abs(smoothed))
    inside = tissue_ref[:, pl.ds(pl.multiple_of(place[3] * width, width), width)] > 0
    soft = jnp.maximum(smoothed, 0.0) + jnp.log1p(small)
    factor_ref[...] = jnp.where(inside, soft, 0.0).astype(jnp.bfloat16)
    sigmoid = jnp.where(smoothed >= 0.0, 1.0, small) / (1.0 + small)
    slope_ref[...] = jnp.where(inside, sigmoid * scale, 0.0)
    weights = jnp.concatenate([own_w[...].astype(jnp.float32), other_w[...].astype(jnp.float32)], axis=1)
    weight_ref[...] = weights.astype(jnp.bfloat16)
    turned_ref[...] = weights.T.astype(jnp.bfloat16)
    genes = own_w.shape[1]
    back_ref[:genes] = column(own_b, genes, 128)
    back_ref[genes:] = column(other_b, genes, 128)


def gene_kernel(
    place, own_f, other_f, keep_ref, came_ref, weight_ref, turned_ref, back_ref, own_p, other_p, load_p, *, step, shift,
):
    width = own_f.shape[1]
    planes = keep_ref.shape[0]
    weights, turned = weight_ref[...], turned_ref[...]
    offset = jnp.concatenate([back_ref[...]] * (step // 128), axis=1)
    load = jnp.zeros(load_p.shape, jnp.float32)
    plane = place[2] ^ shift
    for half, (field, out) in enumerate(((own_f, own_p), (other_f, other_p))):
        row = lax.rem(place[1] + half, 2)
        for at in range(0, width, step):
            f = field[:, at : at + step]
            rate = jnp.dot(turned, f, preferred_element_type=jnp.float32) + offset
            seen = jnp.concatenate(
                [keep_ref[plane, row, :, at : at + step], came_ref[plane, row, :, at : at + step]], axis=0
            ).astype(jnp.float32)
            residual = (1.0 - seen / rate).astype(jnp.bfloat16)
            out[:, at : at + step] = jnp.dot(weights, residual, preferred_element_type=jnp.float32).astype(out.dtype)
            load += lax.dot_general(f, residual, (((1,), (1,)), ((), ())), preferred_element_type=jnp.float32)
    load_p[...] = load


def gene_sums(place, shift, own_f, other_f, keep, came, weights, turned, back):
    factors, width = own_f.shape
    genes = keep.shape[2]
    work = 2 * genes * 2 * width
    return pl.pallas_call(
        functools.partial(gene_kernel, step=1024, shift=shift),
        in_specs=[SMEM] + [VMEM] * 7,
        out_specs=[VMEM] * 3,
        out_shape=[
            jax.ShapeDtypeStruct(own_f.shape, jnp.float32),
            jax.ShapeDtypeStruct(own_f.shape, jnp.bfloat16),
            jax.ShapeDtypeStruct((factors, 2 * genes), jnp.float32),
        ],
        compiler_params=params(12),
        cost_estimate=cost(6 * factors * work, 3 * work, work),
    )(place, own_f, other_f, keep, came, weights, turned, back)


def last_kernel(own_ref, near_ref, far_ref, strength_ref, out_ref):
    factors, width = own_ref.shape
    out_ref[...] = stencil(
        own_ref[...], near_ref[...].astype(jnp.float32), far_ref[...].astype(jnp.float32),
        column(strength_ref, factors, width),
    )


def after(x, *done):
    return lax.optimization_barrier((x, *done))[0]


def local(counts, latent, loading, background, coupling, tissue):
    factors, width = latent.shape
    genes, total_spots = counts.shape
    count = lax.axis_size(SPACE)
    planes = count // 4
    me = lax.axis_index(SPACE)
    place = jnp.stack([me & 1, (me >> 1) & 1, me >> 2, me])

    def send(x, to):
        return lax.ppermute(x, SPACE, [(i, to(i)) for i in range(count)])

    def across(i):
        return i + 1 if i % 2 else i - 1

    def chips(x):
        return lax.ppermute(x, SPACE, [(i, across(i)) for i in range(count) if 0 <= across(i) < count])

    over_core = lambda i: i ^ 1
    over_row = lambda i: i ^ 2
    along = lambda s: lambda i: i ^ (4 * s)

    far = chips(latent)
    near = send(latent, over_core)
    away = cast_counts(place, counts, planes, width, 1)
    keep = cast_counts(place, counts, planes, width, 0)
    other_w, other_b = send(loading, over_core), send(background, over_core)
    strength = coupling.reshape(1, factors)
    full = jax.ShapeDtypeStruct
    field, slope, weights, turned, back = pl.pallas_call(
        functools.partial(factor_kernel, scale=1.0 / (genes * count)),
        in_specs=[SMEM] + [VMEM] * 9,
        out_specs=[VMEM] * 5,
        out_shape=[
            full(latent.shape, jnp.bfloat16), full(latent.shape, jnp.float32),
            full((factors, 2 * genes), jnp.bfloat16), full((2 * genes, factors), jnp.bfloat16),
            full((2 * genes, 128), jnp.float32),
        ],
        compiler_params=params(8),
        cost_estimate=cost(latent.size * 20, latent.size * 18, latent.size * 3),
    )(
        place, latent, near, far, strength, tissue.reshape(1, total_spots),
        loading, other_w, background.reshape(1, genes), other_b.reshape(1, genes),
    )

    came = send(after(away, field), over_core)
    order = [0, 3, 1, 2]
    fields = {s: field if s == 0 else send(field, along(s)) for s in order}
    total = loads = None
    done, returned = [], []
    for at, s in enumerate(order):
        mine = fields[s] if s == 0 else after(fields[s], done[max(0, at - 2)])
        other = send(mine, over_row)
        own_p, other_p, load = gene_sums(place, s, mine, other, keep, came, weights, turned, back)
        done.append(load)
        loads = load if loads is None else loads + load
        if s == 0:
            total, later = own_p, other_p
        else:
            summed = own_p + send(other_p, over_row).astype(jnp.float32)
            returned.append(send(summed.astype(jnp.bfloat16), along(s)))
    total = total + send(after(later, done[-2]), over_row).astype(jnp.float32)
    for r in returned:
        total = total + r.astype(jnp.float32)
    grad_smooth = total * slope
    rounded = grad_smooth.astype(jnp.bfloat16)
    near2, far2 = send(rounded, over_core), chips(rounded)
    grad_latent = pl.pallas_call(
        last_kernel,
        in_specs=[VMEM] * 4,
        out_specs=VMEM,
        out_shape=full(latent.shape, jnp.float32),
        compiler_params=params(8),
        cost_estimate=cost(latent.size * 10, latent.size * 12),
    )(grad_smooth, near2, far2, strength)
    swapped = send(after(loads, grad_smooth)[:, genes:], over_core)
    grad_loading = (loads[:, :genes] + swapped) / total_spots
    return grad_latent, grad_loading


def solution(mesh):
    split = P(None, ("groups", SPACE))
    return jax.shard_map(
        local,
        mesh=mesh,
        in_specs=(P(SPACE, "groups"), split, split, P(("groups", SPACE)), P("groups"), P("groups")),
        out_specs=(split, split),
        check_vma=False,
    )
```

```python
import functools

import jax
import jax.numpy as jnp
from jax import lax
from jax.experimental import pallas as pl
from jax.experimental.pallas import tpu as pltpu
from jax.sharding import PartitionSpec as P

SPACE = "space"
MIB = 1024 * 1024
VMEM = pl.BlockSpec(memory_space=pltpu.VMEM)
SMEM = pl.BlockSpec(memory_space=pltpu.SMEM)


def params(mib):
    return pltpu.CompilerParams(vmem_limit_bytes=mib * MIB)


def cost(flops, nbytes, trans=0):
    return pl.CostEstimate(flops=flops, bytes_accessed=nbytes, transcendentals=trans)


def cast_kernel(place, counts_ref, out_ref, taken, arrived, *, turn):
    planes, rows, _, width = out_ref.shape
    parity = lax.rem(place[0] + turn, 2)
    copies = []
    for block in range(planes * rows):
        start = pl.multiple_of((2 * block + parity) * width, width)
        copies.append(pltpu.make_async_copy(counts_ref.at[:, pl.ds(start, width)], taken.at[block], arrived.at[block]))
        copies[-1].start()
    for block, copy in enumerate(copies):
        copy.wait()
        out_ref[block // rows, block % rows] = taken[block].astype(jnp.float32).astype(jnp.bfloat16)


def cast_counts(place, counts, planes, width, turn):
    genes = counts.shape[0]
    return pl.pallas_call(
        functools.partial(cast_kernel, turn=turn),
        in_specs=[SMEM, pl.BlockSpec(memory_space=pltpu.HBM)],
        out_specs=VMEM,
        out_shape=jax.ShapeDtypeStruct((planes, 2, genes, width), jnp.bfloat16),
        scratch_shapes=[pltpu.VMEM((2 * planes, genes, width), jnp.int32), pltpu.SemaphoreType.DMA((2 * planes,))],
        compiler_params=params(14),
        cost_estimate=cost(counts.size, counts.size * 3),
    )(place, counts)


def column(row_ref, rows, lanes):
    tile = jnp.broadcast_to(row_ref[...], (128, rows)).T
    return jnp.concatenate([tile] * (lanes // 128), axis=1)


def base_kernel(values_ref, near_ref, strength_ref, base_ref, tile_ref):
    factors, width = values_ref.shape
    values = values_ref[...]
    tile = column(strength_ref, factors, 128)
    at = lax.broadcasted_iota(jnp.int32, values.shape, 1)
    left = jnp.where(at > 0, pltpu.roll(values, 1, 1), 0.0)
    right = jnp.where(at < width - 1, pltpu.roll(values, width - 1, 1), 0.0)
    around = near_ref[...].astype(jnp.float32) + left + right - 4.0 * values
    base_ref[...] = values + jnp.concatenate([tile] * (width // 128), axis=1) * around
    tile_ref[...] = tile


def stencil_base(values, near, strength):
    return pl.pallas_call(
        base_kernel,
        in_specs=[VMEM] * 3,
        out_specs=[VMEM] * 2,
        out_shape=[
            jax.ShapeDtypeStruct(values.shape, jnp.float32),
            jax.ShapeDtypeStruct((values.shape[0], 128), jnp.float32),
        ],
        compiler_params=params(8),
        cost_estimate=cost(values.size * 9, values.size * 12),
    )(values, near, strength)


def with_far(base_ref, far_ref, tile_ref):
    wide = jnp.concatenate([tile_ref[...]] * (base_ref.shape[1] // 128), axis=1)
    return base_ref[...] + wide * far_ref[...].astype(jnp.float32)


def weight_kernel(own_w, other_w, own_b, other_b, weight_ref, turned_ref, back_ref):
    weights = jnp.concatenate([own_w[...].astype(jnp.float32), other_w[...].astype(jnp.float32)], axis=1)
    weight_ref[...] = weights.astype(jnp.bfloat16)
    turned_ref[...] = weights.T.astype(jnp.bfloat16)
    genes = own_w.shape[1]
    back_ref[:genes] = column(own_b, genes, 128)
    back_ref[genes:] = column(other_b, genes, 128)


def factor_kernel(place, base_ref, far_ref, tile_ref, tissue_ref, factor_ref, slope_ref, *, scale):
    width = base_ref.shape[1]
    smoothed = with_far(base_ref, far_ref, tile_ref)
    small = jnp.exp(-jnp.abs(smoothed))
    inside = tissue_ref[:, pl.ds(pl.multiple_of(place[3] * width, width), width)] > 0
    soft = jnp.maximum(smoothed, 0.0) + jnp.log1p(small)
    factor_ref[...] = jnp.where(inside, soft, 0.0).astype(jnp.bfloat16)
    sigmoid = jnp.where(smoothed >= 0.0, 1.0, small) / (1.0 + small)
    slope_ref[...] = jnp.where(inside, sigmoid * scale, 0.0)


def gene_kernel(
    place, own_f, other_f, keep_ref, came_ref, weight_ref, turned_ref, back_ref, own_p, other_p, load_p, *, step, shift,
):
    width = own_f.shape[1]
    planes = keep_ref.shape[0]
    weights, turned = weight_ref[...], turned_ref[...]
    offset = jnp.concatenate([back_ref[...]] * (step // 128), axis=1)
    load = jnp.zeros(load_p.shape, jnp.float32)
    plane = place[2] ^ shift
    for half, (field, out) in enumerate(((own_f, own_p), (other_f, other_p))):
        row = lax.rem(place[1] + half, 2)
        for at in range(0, width, step):
            f = field[:, at : at + step]
            rate = jnp.dot(turned, f, preferred_element_type=jnp.float32) + offset
            seen = jnp.concatenate(
                [keep_ref[plane, row, :, at : at + step], came_ref[plane, row, :, at : at + step]], axis=0
            ).astype(jnp.float32)
            residual = (1.0 - seen / rate).astype(jnp.bfloat16)
            out[:, at : at + step] = jnp.dot(weights, residual, preferred_element_type=jnp.float32).astype(out.dtype)
            load += lax.dot_general(f, residual, (((1,), (1,)), ((), ())), preferred_element_type=jnp.float32)
    load_p[...] = load


def gene_sums(place, shift, own_f, other_f, keep, came, weights, turned, back, kinds):
    factors, width = own_f.shape
    genes = keep.shape[2]
    work = 2 * genes * 2 * width
    return pl.pallas_call(
        functools.partial(gene_kernel, step=1024, shift=shift),
        in_specs=[SMEM] + [VMEM] * 7,
        out_specs=[VMEM] * 3,
        out_shape=[
            jax.ShapeDtypeStruct(own_f.shape, kinds[0]),
            jax.ShapeDtypeStruct(own_f.shape, kinds[1]),
            jax.ShapeDtypeStruct((factors, 2 * genes), jnp.float32),
        ],
        compiler_params=params(12),
        cost_estimate=cost(6 * factors * work, 3 * work, work),
    )(place, own_f, other_f, keep, came, weights, turned, back)


def last_kernel(base_ref, far_ref, tile_ref, out_ref):
    out_ref[...] = with_far(base_ref, far_ref, tile_ref)


def after(x, *done):
    return lax.optimization_barrier((x, *done))[0]


def local(counts, latent, loading, background, coupling, tissue):
    factors, width = latent.shape
    genes, total_spots = counts.shape
    count = lax.axis_size(SPACE)
    planes = count // 4
    me = lax.axis_index(SPACE)
    place = jnp.stack([me & 1, (me >> 1) & 1, me >> 2, me])

    def send(x, to):
        return lax.ppermute(x, SPACE, [(i, to(i)) for i in range(count)])

    def across(i):
        return i + 1 if i % 2 else i - 1

    def chips(x):
        return lax.ppermute(x, SPACE, [(i, across(i)) for i in range(count) if 0 <= across(i) < count])

    over_core = lambda i: i ^ 1
    over_row = lambda i: i ^ 2
    along = lambda s: lambda i: i ^ (4 * s)

    ready = after(latent, place)
    far = chips(ready)
    near = send(ready, over_core)
    away = cast_counts(place, counts, planes, width, 1)
    keep = cast_counts(place, counts, planes, width, 0)
    other_w, other_b = send(loading, over_core), send(background, over_core)
    strength = coupling.reshape(1, factors)
    full = jax.ShapeDtypeStruct
    base, tile = stencil_base(latent, near, strength)
    weights, turned, back = pl.pallas_call(
        weight_kernel,
        in_specs=[VMEM] * 4,
        out_specs=[VMEM] * 3,
        out_shape=[
            full((factors, 2 * genes), jnp.bfloat16), full((2 * genes, factors), jnp.bfloat16),
            full((2 * genes, 128), jnp.float32),
        ],
        compiler_params=params(8),
        cost_estimate=cost(genes * 128, genes * 1024),
    )(loading, other_w, background.reshape(1, genes), other_b.reshape(1, genes))
    field, slope = pl.pallas_call(
        functools.partial(factor_kernel, scale=1.0 / (genes * count)),
        in_specs=[SMEM] + [VMEM] * 4,
        out_specs=[VMEM] * 2,
        out_shape=[full(latent.shape, jnp.bfloat16), full(latent.shape, jnp.float32)],
        compiler_params=params(8),
        cost_estimate=cost(latent.size * 20, latent.size * 18, latent.size * 3),
    )(after(place, keep, weights), base, far, tile, tissue.reshape(1, total_spots))
    came = send(after(away, field), over_core)

    order = [0, 1, 2, 3]
    send_ties, kernel_ties, sum_ties = {3: (('K', 0),), 2: (('K', 0),)}, {}, {}
    marks = {}
    held = lambda x, names: after(x, *[marks[n] for n in names if n in marks]) if names else x
    narrow, full_width = jnp.bfloat16, jnp.float32
    fields = {s: field if s == 0 else send(field, along(s)) for s in order}
    for s in order:
        marks["G", s] = fields[s]
    others = {0: send(field, over_row)}
    marks["H", 0] = others[0]
    loads = None
    sums = {}
    for s in order:
        if s == 1:
            others[1] = send(others[0], along(1))
        elif s:
            others[s] = send(held(fields[s], send_ties.get(s, ())), over_row)
        kinds = (full_width if s != 1 else narrow, full_width if s == 0 else narrow)
        own_p, other_p, load = gene_sums(
            held(place, kernel_ties.get(s, ())), s, fields[s], others[s], keep, came, weights, turned, back, kinds
        )
        marks["K", s] = load
        loads = load if loads is None else loads + load
        sums[s] = own_p, other_p
    own_0 = sums[0][0] + send(sums[1][0], along(1)).astype(jnp.float32)
    other_0 = sums[0][1] + send(sums[1][1], along(1)).astype(jnp.float32)
    total = own_0 + send(held(other_0.astype(jnp.bfloat16), sum_ties.get(0, ())), over_row).astype(jnp.float32)
    marks["S", 0] = total
    for s in order:
        if s > 1:
            own_p, other_p = sums[s]
            summed = own_p + send(held(other_p, sum_ties.get(s, ())), over_row).astype(jnp.float32)
            total = total + send(summed.astype(jnp.bfloat16), along(s)).astype(jnp.float32)
    grad_smooth = total * slope
    swapped = send(after(loads, grad_smooth)[:, genes:], over_core)
    rounded = grad_smooth.astype(jnp.bfloat16)
    far2 = chips(rounded)
    near2 = send(after(rounded, swapped), over_core)
    base2, tile2 = stencil_base(grad_smooth, near2, strength)
    grad_latent = pl.pallas_call(
        last_kernel,
        in_specs=[VMEM] * 3,
        out_specs=VMEM,
        out_shape=full(latent.shape, jnp.float32),
        compiler_params=params(8),
        cost_estimate=cost(latent.size * 10, latent.size * 12),
    )(base2, far2, tile2)
    grad_loading = (loads[:, :genes] + swapped) / total_spots
    return grad_latent, grad_loading


def solution(mesh):
    split = P(None, ("groups", SPACE))
    return jax.shard_map(
        local,
        mesh=mesh,
        in_specs=(P(SPACE, "groups"), split, split, P(("groups", SPACE)), P("groups"), P("groups")),
        out_specs=(split, split),
        check_vma=False,
    )
```

```python
import functools

import jax
import jax.numpy as jnp
from jax import lax
from jax.experimental import pallas as pl
from jax.experimental.pallas import tpu as pltpu
from jax.sharding import PartitionSpec as P

SPACE = "space"
MIB = 1024 * 1024
VMEM = pl.BlockSpec(memory_space=pltpu.VMEM)


def params(mib):
    return pltpu.CompilerParams(vmem_limit_bytes=mib * MIB)


def cost(flops, nbytes, trans=0):
    return pl.CostEstimate(flops=flops, bytes_accessed=nbytes, transcendentals=trans)


def cast_kernel(counts_ref, out_ref, taken, arrived, *, turn):
    planes, rows, _, width = out_ref.shape
    parity = (lax.axis_index(SPACE) + turn) & 1
    copies = []
    for block in range(planes * rows):
        start = pl.multiple_of((2 * block + parity) * width, width)
        copies.append(pltpu.make_async_copy(counts_ref.at[:, pl.ds(start, width)], taken.at[block], arrived.at[block]))
        copies[-1].start()
    for block, copy in enumerate(copies):
        copy.wait()
        out_ref[block // rows, block % rows] = taken[block].astype(jnp.float32).astype(jnp.bfloat16)


def cast_counts(counts, planes, width, turn):
    genes = counts.shape[0]
    return pl.pallas_call(
        functools.partial(cast_kernel, turn=turn),
        in_specs=[pl.BlockSpec(memory_space=pltpu.HBM)],
        out_specs=VMEM,
        out_shape=jax.ShapeDtypeStruct((planes, 2, genes, width), jnp.bfloat16),
        scratch_shapes=[pltpu.VMEM((2 * planes, genes, width), jnp.int32), pltpu.SemaphoreType.DMA((2 * planes,))],
        compiler_params=params(14),
        cost_estimate=cost(counts.size, counts.size * 3),
    )(counts)


def column(row_ref, rows, lanes):
    tile = jnp.broadcast_to(row_ref[...], (128, rows)).T
    return jnp.concatenate([tile] * (lanes // 128), axis=1)


def base_kernel(values_ref, near_ref, strength_ref, base_ref, tile_ref):
    factors, width = values_ref.shape
    values = values_ref[...]
    tile = column(strength_ref, factors, 128)
    at = lax.broadcasted_iota(jnp.int32, values.shape, 1)
    left = jnp.where(at > 0, pltpu.roll(values, 1, 1), 0.0)
    right = jnp.where(at < width - 1, pltpu.roll(values, width - 1, 1), 0.0)
    around = near_ref[...].astype(jnp.float32) + left + right - 4.0 * values
    base_ref[...] = values + jnp.concatenate([tile] * (width // 128), axis=1) * around
    tile_ref[...] = tile


def stencil_base(values, near, strength):
    return pl.pallas_call(
        base_kernel,
        in_specs=[VMEM] * 3,
        out_specs=[VMEM] * 2,
        out_shape=[
            jax.ShapeDtypeStruct(values.shape, jnp.float32),
            jax.ShapeDtypeStruct((values.shape[0], 128), jnp.float32),
        ],
        compiler_params=params(8),
        cost_estimate=cost(values.size * 9, values.size * 12),
    )(values, near, strength)


def with_far(base_ref, far_ref, tile_ref):
    wide = jnp.concatenate([tile_ref[...]] * (base_ref.shape[1] // 128), axis=1)
    return base_ref[...] + wide * far_ref[...].astype(jnp.float32)


def weight_kernel(own_w, other_w, own_b, other_b, weight_ref, turned_ref, back_ref):
    weights = jnp.concatenate([own_w[...].astype(jnp.float32), other_w[...].astype(jnp.float32)], axis=1)
    weight_ref[...] = weights.astype(jnp.bfloat16)
    turned_ref[...] = weights.T.astype(jnp.bfloat16)
    genes = own_w.shape[1]
    back_ref[:genes] = column(own_b, genes, 128)
    back_ref[genes:] = column(other_b, genes, 128)


def factor_kernel(base_ref, far_ref, tile_ref, tissue_ref, factor_ref, slope_ref, *, scale):
    width = base_ref.shape[1]
    smoothed = with_far(base_ref, far_ref, tile_ref)
    small = jnp.exp(-jnp.abs(smoothed))
    inside = tissue_ref[:, pl.ds(pl.multiple_of(lax.axis_index(SPACE) * width, width), width)] > 0
    soft = jnp.maximum(smoothed, 0.0) + jnp.log1p(small)
    factor_ref[...] = jnp.where(inside, soft, 0.0).astype(jnp.bfloat16)
    sigmoid = jnp.where(smoothed >= 0.0, 1.0, small) / (1.0 + small)
    slope_ref[...] = jnp.where(inside, sigmoid * scale, 0.0)


def gene_kernel(
    own_f, other_f, keep_ref, came_ref, weight_ref, turned_ref, back_ref, own_p, other_p, load_p, *, step, shift,
):
    width = own_f.shape[1]
    planes = keep_ref.shape[0]
    weights, turned = weight_ref[...], turned_ref[...]
    offset = jnp.concatenate([back_ref[...]] * (step // 128), axis=1)
    load = jnp.zeros(load_p.shape, jnp.float32)
    me = lax.axis_index(SPACE)
    plane = (me >> 2) ^ shift
    for half, (field, out) in enumerate(((own_f, own_p), (other_f, other_p))):
        row = ((me >> 1) + half) & 1
        for at in range(0, width, step):
            f = field[:, at : at + step]
            rate = jnp.dot(turned, f, preferred_element_type=jnp.float32) + offset
            seen = jnp.concatenate(
                [keep_ref[plane, row, :, at : at + step], came_ref[plane, row, :, at : at + step]], axis=0
            ).astype(jnp.float32)
            residual = (1.0 - seen / rate).astype(jnp.bfloat16)
            out[:, at : at + step] = jnp.dot(weights, residual, preferred_element_type=jnp.float32).astype(out.dtype)
            load += lax.dot_general(f, residual, (((1,), (1,)), ((), ())), preferred_element_type=jnp.float32)
    load_p[...] = load


def gene_sums(shift, own_f, other_f, keep, came, weights, turned, back, kinds):
    factors, width = own_f.shape
    genes = keep.shape[2]
    work = 2 * genes * 2 * width
    return pl.pallas_call(
        functools.partial(gene_kernel, step=1024, shift=shift),
        in_specs=[VMEM] * 7,
        out_specs=[VMEM] * 3,
        out_shape=[
            jax.ShapeDtypeStruct(own_f.shape, kinds[0]),
            jax.ShapeDtypeStruct(own_f.shape, kinds[1]),
            jax.ShapeDtypeStruct((factors, 2 * genes), jnp.float32),
        ],
        compiler_params=params(12),
        cost_estimate=cost(6 * factors * work, 3 * work, work),
    )(own_f, other_f, keep, came, weights, turned, back)


def last_kernel(base_ref, far_ref, tile_ref, out_ref):
    out_ref[...] = with_far(base_ref, far_ref, tile_ref)


def after(x, *done):
    return lax.optimization_barrier((x, *done))[0]


def local(counts, latent, loading, background, coupling, tissue):
    factors, width = latent.shape
    genes, total_spots = counts.shape
    count = lax.axis_size(SPACE)
    planes = count // 4

    def send(x, to):
        return lax.ppermute(x, SPACE, [(i, to(i)) for i in range(count)])

    def across(i):
        return i + 1 if i % 2 else i - 1

    def chips(x):
        return lax.ppermute(x, SPACE, [(i, across(i)) for i in range(count) if 0 <= across(i) < count])

    over_core = lambda i: i ^ 1
    over_row = lambda i: i ^ 2
    along = lambda s: lambda i: i ^ 4 * s

    far = chips(latent)
    near = send(latent, over_core)
    away = cast_counts(counts, planes, width, 1)
    keep = cast_counts(counts, planes, width, 0)
    other_w, other_b = send(loading, over_core), send(background, over_core)
    strength = coupling.reshape(1, factors)
    full = jax.ShapeDtypeStruct
    base, tile = stencil_base(latent, near, strength)
    weights, turned, back = pl.pallas_call(
        weight_kernel,
        in_specs=[VMEM] * 4,
        out_specs=[VMEM] * 3,
        out_shape=[
            full((factors, 2 * genes), jnp.bfloat16), full((2 * genes, factors), jnp.bfloat16),
            full((2 * genes, 128), jnp.float32),
        ],
        compiler_params=params(8),
        cost_estimate=cost(genes * 128, genes * 1024),
    )(loading, other_w, background.reshape(1, genes), other_b.reshape(1, genes))
    field, slope = pl.pallas_call(
        functools.partial(factor_kernel, scale=1.0 / (genes * count)),
        in_specs=[VMEM] * 4,
        out_specs=[VMEM] * 2,
        out_shape=[full(latent.shape, jnp.bfloat16), full(latent.shape, jnp.float32)],
        compiler_params=params(8),
        cost_estimate=cost(latent.size * 20, latent.size * 18, latent.size * 3),
    )(after(base, keep, weights), far, tile, tissue.reshape(1, total_spots))
    came = send(after(away, field), over_core)

    fields = {s: field if s == 0 else send(field, along(s)) for s in range(planes)}
    others = {0: send(field, over_row)}
    sums = {}
    loads = None
    for s in range(planes):
        if s == 1:
            others[1] = send(others[0], along(1))
        elif s:
            others[s] = send(after(fields[s], sums[0][2]), over_row)
        kinds = {0: (jnp.float32, jnp.float32), 1: (jnp.bfloat16, jnp.bfloat16)}.get(s, (jnp.float32, jnp.bfloat16))
        sums[s] = gene_sums(s, fields[s], others[s], keep, came, weights, turned, back, kinds)
        loads = sums[s][2] if loads is None else loads + sums[s][2]
    own_0 = sums[0][0] + send(sums[1][0], along(1)).astype(jnp.float32)
    other_0 = (sums[0][1] + send(sums[1][1], along(1)).astype(jnp.float32)).astype(jnp.bfloat16)
    total = own_0 + send(other_0, over_row).astype(jnp.float32)
    for s in range(2, planes):
        summed = sums[s][0] + send(sums[s][1], over_row).astype(jnp.float32)
        total = total + send(summed.astype(jnp.bfloat16), along(s)).astype(jnp.float32)
    grad_smooth = total * slope
    swapped = send(after(loads, grad_smooth)[:, genes:], over_core)
    rounded = grad_smooth.astype(jnp.bfloat16)
    far2 = chips(rounded)
    near2 = send(after(rounded, swapped), over_core)
    base2, tile2 = stencil_base(grad_smooth, near2, strength)
    grad_latent = pl.pallas_call(
        last_kernel,
        in_specs=[VMEM] * 3,
        out_specs=VMEM,
        out_shape=full(latent.shape, jnp.float32),
        compiler_params=params(8),
        cost_estimate=cost(latent.size * 10, latent.size * 12),
    )(base2, far2, tile2)
    grad_loading = (loads[:, :genes] + swapped) / total_spots
    return grad_latent, grad_loading


def solution(mesh):
    split = P(None, ("groups", SPACE))
    return jax.shard_map(
        local,
        mesh=mesh,
        in_specs=(P(SPACE, "groups"), split, split, P(("groups", SPACE)), P("groups"), P("groups")),
        out_specs=(split, split),
        check_vma=False,
    )
```

```python
import functools

import jax
import jax.numpy as jnp
from jax import lax
from jax.experimental import pallas as pl
from jax.experimental.pallas import tpu as pltpu
from jax.sharding import PartitionSpec as P

SPACE = "space"
MIB = 1024 * 1024
STEPS = 8191.0
VMEM = pl.BlockSpec(memory_space=pltpu.VMEM)


def params(mib):
    return pltpu.CompilerParams(vmem_limit_bytes=mib * MIB)


def cost(flops, nbytes, trans=0):
    return pl.CostEstimate(flops=flops, bytes_accessed=nbytes, transcendentals=trans)


def cast_kernel(counts_ref, out_ref, taken, arrived, *, turn):
    planes, rows, _, width = out_ref.shape
    parity = (lax.axis_index(SPACE) + turn) & 1
    copies = []
    for block in range(planes * rows):
        start = pl.multiple_of((2 * block + parity) * width, width)
        copies.append(pltpu.make_async_copy(counts_ref.at[:, pl.ds(start, width)], taken.at[block], arrived.at[block]))
        copies[-1].start()
    for block, copy in enumerate(copies):
        copy.wait()
        out_ref[block // rows, block % rows] = taken[block].astype(jnp.float32).astype(jnp.bfloat16)


def cast_counts(counts, planes, width, turn):
    genes = counts.shape[0]
    return pl.pallas_call(
        functools.partial(cast_kernel, turn=turn),
        in_specs=[pl.BlockSpec(memory_space=pltpu.HBM)],
        out_specs=VMEM,
        out_shape=jax.ShapeDtypeStruct((planes, 2, genes, width), jnp.bfloat16),
        scratch_shapes=[pltpu.VMEM((2 * planes, genes, width), jnp.int32), pltpu.SemaphoreType.DMA((2 * planes,))],
        compiler_params=params(14),
        cost_estimate=cost(counts.size, counts.size * 3),
    )(counts)


def column(row_ref, rows, lanes):
    tile = jnp.broadcast_to(row_ref[...], (128, rows)).T
    return jnp.concatenate([tile] * (lanes // 128), axis=1)


def base_kernel(values_ref, near_ref, strength_ref, base_ref, tile_ref):
    factors, width = values_ref.shape
    values = values_ref[...]
    tile = column(strength_ref, factors, 128)
    at = lax.broadcasted_iota(jnp.int32, values.shape, 1)
    left = jnp.where(at > 0, pltpu.roll(values, 1, 1), 0.0)
    right = jnp.where(at < width - 1, pltpu.roll(values, width - 1, 1), 0.0)
    around = near_ref[...].astype(jnp.float32) + left + right - 4.0 * values
    base_ref[...] = values + jnp.concatenate([tile] * (width // 128), axis=1) * around
    tile_ref[...] = tile


def stencil_base(values, near, strength):
    return pl.pallas_call(
        base_kernel,
        in_specs=[VMEM] * 3,
        out_specs=[VMEM] * 2,
        out_shape=[
            jax.ShapeDtypeStruct(values.shape, jnp.float32),
            jax.ShapeDtypeStruct((values.shape[0], 128), jnp.float32),
        ],
        compiler_params=params(8),
        cost_estimate=cost(values.size * 9, values.size * 12),
    )(values, near, strength)


def code_kernel(values_ref, out_ref):
    out_ref[...] = jnp.round(values_ref[...] * STEPS).astype(jnp.int32).astype(jnp.int16)


def with_far(base_ref, far_ref, tile_ref, step=1.0):
    wide = jnp.concatenate([tile_ref[...] * step] * (base_ref.shape[1] // 128), axis=1)
    return base_ref[...] + wide * far_ref[...].astype(jnp.float32)


def weight_kernel(own_w, other_w, own_b, other_b, weight_ref, turned_ref, back_ref):
    weights = jnp.concatenate([own_w[...].astype(jnp.float32), other_w[...].astype(jnp.float32)], axis=1)
    weight_ref[...] = weights.astype(jnp.bfloat16)
    turned_ref[...] = weights.T.astype(jnp.bfloat16)
    genes = own_w.shape[1]
    back_ref[:genes] = column(own_b, genes, 128)
    back_ref[genes:] = column(other_b, genes, 128)


def factor_kernel(base_ref, far_ref, tile_ref, tissue_ref, factor_ref, slope_ref, *, scale):
    width = base_ref.shape[1]
    smoothed = with_far(base_ref, far_ref, tile_ref, 1.0 / STEPS)
    small = jnp.exp(-jnp.abs(smoothed))
    inside = tissue_ref[:, pl.ds(pl.multiple_of(lax.axis_index(SPACE) * width, width), width)] > 0
    soft = jnp.maximum(smoothed, 0.0) + jnp.log1p(small)
    factor_ref[...] = jnp.where(inside, soft, 0.0).astype(jnp.bfloat16)
    sigmoid = jnp.where(smoothed >= 0.0, 1.0, small) / (1.0 + small)
    slope_ref[...] = jnp.where(inside, sigmoid * scale, 0.0)


def gene_kernel(
    own_f, other_f, keep_ref, came_ref, weight_ref, turned_ref, back_ref, own_p, other_p, load_p, *, step, shift,
):
    width = own_f.shape[1]
    planes = keep_ref.shape[0]
    weights, turned = weight_ref[...], turned_ref[...]
    offset = jnp.concatenate([back_ref[...]] * (step // 128), axis=1)
    load = jnp.zeros(load_p.shape, jnp.float32)
    me = lax.axis_index(SPACE)
    plane = (me >> 2) ^ shift
    for half, (field, out) in enumerate(((own_f, own_p), (other_f, other_p))):
        row = ((me >> 1) + half) & 1
        for at in range(0, width, step):
            f = field[:, at : at + step]
            rate = jnp.dot(turned, f, preferred_element_type=jnp.float32) + offset
            seen = jnp.concatenate(
                [keep_ref[plane, row, :, at : at + step], came_ref[plane, row, :, at : at + step]], axis=0
            ).astype(jnp.float32)
            residual = (1.0 - seen / rate).astype(jnp.bfloat16)
            out[:, at : at + step] = jnp.dot(weights, residual, preferred_element_type=jnp.float32).astype(out.dtype)
            load += lax.dot_general(f, residual, (((1,), (1,)), ((), ())), preferred_element_type=jnp.float32)
    load_p[...] = load


def gene_sums(shift, own_f, other_f, keep, came, weights, turned, back, kinds):
    factors, width = own_f.shape
    genes = keep.shape[2]
    work = 2 * genes * 2 * width
    return pl.pallas_call(
        functools.partial(gene_kernel, step=1024, shift=shift),
        in_specs=[VMEM] * 7,
        out_specs=[VMEM] * 3,
        out_shape=[
            jax.ShapeDtypeStruct(own_f.shape, kinds[0]),
            jax.ShapeDtypeStruct(own_f.shape, kinds[1]),
            jax.ShapeDtypeStruct((factors, 2 * genes), jnp.float32),
        ],
        compiler_params=params(12),
        cost_estimate=cost(6 * factors * work, 3 * work, work),
    )(own_f, other_f, keep, came, weights, turned, back)


def last_kernel(base_ref, far_ref, tile_ref, out_ref):
    out_ref[...] = with_far(base_ref, far_ref, tile_ref)


def after(x, *done):
    return lax.optimization_barrier((x, *done))[0]


def local(counts, latent, loading, background, coupling, tissue):
    factors, width = latent.shape
    genes, total_spots = counts.shape
    count = lax.axis_size(SPACE)
    planes = count // 4

    def send(x, to):
        return lax.ppermute(x, SPACE, [(i, to(i)) for i in range(count)])

    def across(i):
        return i + 1 if i % 2 else i - 1

    def chips(x):
        return lax.ppermute(x, SPACE, [(i, across(i)) for i in range(count) if 0 <= across(i) < count])

    over_core = lambda i: i ^ 1
    over_row = lambda i: i ^ 2
    along = lambda s: lambda i: i ^ 4 * s

    coded = pl.pallas_call(
        code_kernel,
        in_specs=[VMEM],
        out_specs=VMEM,
        out_shape=jax.ShapeDtypeStruct(latent.shape, jnp.int16),
        compiler_params=params(8),
        cost_estimate=cost(latent.size * 2, latent.size * 6),
    )(latent)
    far = chips(coded)
    near = send(latent, over_core)
    away = cast_counts(counts, planes, width, 1)
    keep = cast_counts(counts, planes, width, 0)
    other_w, other_b = send(loading, over_core), send(background, over_core)
    strength = coupling.reshape(1, factors)
    full = jax.ShapeDtypeStruct
    base, tile = stencil_base(latent, near, strength)
    weights, turned, back = pl.pallas_call(
        weight_kernel,
        in_specs=[VMEM] * 4,
        out_specs=[VMEM] * 3,
        out_shape=[
            full((factors, 2 * genes), jnp.bfloat16), full((2 * genes, factors), jnp.bfloat16),
            full((2 * genes, 128), jnp.float32),
        ],
        compiler_params=params(8),
        cost_estimate=cost(genes * 128, genes * 1024),
    )(loading, other_w, background.reshape(1, genes), other_b.reshape(1, genes))
    field, slope = pl.pallas_call(
        functools.partial(factor_kernel, scale=1.0 / (genes * count)),
        in_specs=[VMEM] * 4,
        out_specs=[VMEM] * 2,
        out_shape=[full(latent.shape, jnp.bfloat16), full(latent.shape, jnp.float32)],
        compiler_params=params(8),
        cost_estimate=cost(latent.size * 20, latent.size * 18, latent.size * 3),
    )(after(base, weights), far, tile, tissue.reshape(1, total_spots))
    came = send(after(away, field), over_core)

    fields = {s: field if s == 0 else send(field, along(s)) for s in range(planes)}
    others = {0: send(field, over_row)}
    sums = {}
    loads = None
    for s in range(planes):
        if s == 1:
            others[1] = send(others[0], along(1))
        elif s:
            others[s] = send(after(fields[s], sums[0][2]), over_row)
        kinds = {0: (jnp.float32, jnp.float32), 1: (jnp.bfloat16, jnp.bfloat16)}.get(s, (jnp.float32, jnp.bfloat16))
        sums[s] = gene_sums(s, fields[s], others[s], keep, came, weights, turned, back, kinds)
        loads = sums[s][2] if loads is None else loads + sums[s][2]
    own_0 = sums[0][0] + send(sums[1][0], along(1)).astype(jnp.float32)
    other_0 = (sums[0][1] + send(sums[1][1], along(1)).astype(jnp.float32)).astype(jnp.bfloat16)
    total = own_0 + send(other_0, over_row).astype(jnp.float32)
    for s in range(2, planes):
        summed = sums[s][0] + send(sums[s][1], over_row).astype(jnp.float32)
        total = total + send(summed.astype(jnp.bfloat16), along(s)).astype(jnp.float32)
    grad_smooth = total * slope
    swapped = send(after(loads, grad_smooth)[:, genes:], over_core)
    rounded = grad_smooth.astype(jnp.bfloat16)
    far2 = chips(rounded)
    near2 = send(after(rounded, swapped), over_core)
    base2, tile2 = stencil_base(grad_smooth, near2, strength)
    grad_latent = pl.pallas_call(
        last_kernel,
        in_specs=[VMEM] * 3,
        out_specs=VMEM,
        out_shape=full(latent.shape, jnp.float32),
        compiler_params=params(8),
        cost_estimate=cost(latent.size * 10, latent.size * 12),
    )(base2, far2, tile2)
    grad_loading = (loads[:, :genes] + swapped) / total_spots
    return grad_latent, grad_loading


def solution(mesh):
    split = P(None, ("groups", SPACE))
    return jax.shard_map(
        local,
        mesh=mesh,
        in_specs=(P(SPACE, "groups"), split, split, P(("groups", SPACE)), P("groups"), P("groups")),
        out_specs=(split, split),
        check_vma=False,
    )
```
